32 devices in a mesh: grp: 4 (over y, core), dev: 8 (over z, x).
Axes of the slice: x: 2, y: 2, z: 4, core: 2. Of those that a mesh axis runs over, the one named last changes fastest.
Arguments:
- tiles: bfloat16 [4, 8192, 4096], P('grp', 'dev'), may hold values from -0.75 to 0.75
- owner: int32 [4, 8192, 1], P('grp', 'dev'), may hold values from 0 to 7; in each aligned block of 1024 rows (0 to 1023, 1024 to 2047, ..., all dimensions but the last counted through in order) at most 256 rows name the same one
- target: int32 [4, 8192], P('grp', 'dev'), may hold values from 0 to 159
- mass: float32 [4, 16384], P('grp', 'dev'), may hold values from 30 to 100
- rhs: float32 [4, 16384], P('grp', 'dev'), may hold values from -1200 to 1200
- faces: int32 [4, 4, 256], P(None, 'grp', 'dev'), may hold values from 0 to 31, as said below
Outputs:
- smoothed: float32 [4, 16384], P('grp', 'dev')
The draws below stay inside these ranges and needn't reach their ends.
Inputs may be any that keep to these rules, and one draw needn't show every extreme that they name: At most 256 tiles of one device have the same owner. `faces`: each entry names a row block of another colour than its own row block.
All inputs are finite; a program needn't handle non-finite values.
Results may differ from the reference program's by a relative error of at most 0.0003.
Values may be sent and summed in bfloat16 or wider, within the bound.
A program may use at most 128 MiB of HBM per device.

```python
import math
import jax
import jax.numpy as jnp
import numpy as np
from jax import lax

BLK = 64
COLOURS = 4
SWEEPS = 2
COLBLK = 8
TILES = 1024
ROWBLK = 32
CAP = 256
ROWS = 256
ELEMS = 8192
N_GRP = 4
N_DEV = 8


def draw_faces(key, part):
    key = jax.random.fold_in(key, 7)
    first, second = jax.random.split(key)
    local = jnp.arange(N_DEV * ROWBLK, dtype=jnp.int32) % ROWBLK
    colour = (local // COLBLK)[None, None, :]
    step = jax.random.randint(first, (4, N_GRP, N_DEV * ROWBLK), 1, 4, dtype=jnp.int32)
    within = jax.random.randint(second, (4, N_GRP, N_DEV * ROWBLK), 0, COLBLK, dtype=jnp.int32)
    return ((colour + step) % 4 * COLBLK + within).astype(jnp.int32)


def draw_tiles(key, part):
    key = jax.random.fold_in(key, 11)
    shape = (N_GRP, ELEMS, BLK * BLK)
    values = 0.3 * jax.random.truncated_normal(key, -2.5, 2.5, shape, jnp.float32)
    return values.astype(jnp.bfloat16)


def draw_rhs(key, part):
    key = jax.random.fold_in(key, 13)
    shape = (N_GRP, ROWS * BLK)
    values = 200.0 * jax.random.truncated_normal(key, -6.0, 6.0, shape, jnp.float32)
    return values.astype(jnp.float32)


def set_ends(result, own_key, smallest, largest):
    index_at = [jax.random.randint(jax.random.fold_in(own_key, axis), (), 0, length) for axis, length in enumerate(result.shape)]
    main_axis = result.shape.index(max(result.shape))
    beside = index_at[:main_axis] + [(index_at[main_axis] + 1) % result.shape[main_axis]] + index_at[main_axis + 1:]
    return result.at[tuple(index_at)].set(smallest).at[tuple(beside)].set(largest)


def block_scale(stream_key, shape, shards, smallest, largest):
    level = 1.0
    for position, parts in shards:
        heights = jax.random.uniform(jax.random.fold_in(jax.random.fold_in(stream_key, 6), position), (parts,), jnp.float32, smallest / len(shards), largest / len(shards))
        level = level * jnp.repeat(jnp.exp(heights), shape[position] // parts).reshape((-1,) + (1,) * (len(shape) - 1 - position))
    return level


def assign_block(rng, own, number, rows, number_of, top, reach, lean):
    ranking = jax.random.permutation(rng, number_of)
    packed, common = load_shares(number_of, rows * top, reach, lean, True), load_shares(number_of, rows * top, reach, lean, False)
    places = jnp.arange(number_of)

    def named(lengths, turn):
        used = int((lengths > 0).sum())
        fixed = max(1, used // 4)
        passed = fixed + (places - fixed + turn * (used - fixed)) % max(1, number_of - fixed)
        return jnp.zeros((number_of,), jnp.int32).at[ranking[jnp.where(places < fixed, places, passed)]].set(jnp.asarray(lengths, jnp.int32))

    lengths = jnp.where(number % 4 == 0, named(packed, number // 4), named(common, number - number // 4 - 1))
    mixed = jax.random.permutation(jax.random.fold_in(own, 3), number_of)
    giver, taker = mixed[0:number_of // 2 * 2:2], mixed[1:number_of // 2 * 2:2]
    slack = jnp.minimum(lengths[giver] - 1, reach - lengths[taker]) // 2
    slack = jnp.where((giver == ranking[0]) | (taker == ranking[0]) | (lengths[taker] == 0), 0, jnp.maximum(slack, 0))
    passed = jax.random.randint(jax.random.fold_in(own, 4), (number_of // 2,), 0, 1 << 20) % (slack + 1)
    lengths = lengths.at[giver].add(-passed).at[taker].add(passed)
    items = jnp.searchsorted(jnp.cumsum(lengths), jnp.arange(rows * top), side="right").astype(jnp.int32)
    listing = items.reshape(top, rows).T
    listing = listing[jax.random.permutation(jax.random.fold_in(own, 1), rows)]
    turn = jax.random.randint(jax.random.fold_in(own, 2), (rows, 1), 0, top)
    return jnp.take_along_axis(listing, (jnp.arange(top)[None, :] + turn) % top, axis=1)


def load_shares(count, total, bound, lean, full):
    weights = [(1 << 20) // math.isqrt(rank ** lean) + 1 for rank in range(1, count + 1)]
    largest = bound if full else min(bound, max(-(-total // count), total * weights[0] // sum(weights)))
    least = 1 if total - largest >= count - 1 else 0
    given, surplus = [largest] + [least] * (count - 1), total - largest - least * (count - 1)
    while surplus > 0:
        movable = [i for i in range(1, count) if given[i] < largest] or [i for i in range(1, count) if given[i] < bound]
        whole, budget = sum([weights[i] for i in movable]), surplus
        for i in movable:
            extra = min(bound - given[i], max(1, budget * weights[i] // whole), surplus)
            given[i] = given[i] + extra
            surplus = surplus - extra
    return np.array(given)


def setup_inputs(seed: int = 0) -> dict:
    keys = jax.random.split(jax.random.key(seed), 7)
    tiles = draw_tiles(jax.random.fold_in(keys[6], 71), 0)
    owner_keys = jax.random.split(jax.random.fold_in(keys[1], 1), N_GRP * ELEMS // TILES)
    owner_turns = jax.random.permutation(jax.random.fold_in(keys[1], 3), N_GRP * ELEMS // TILES)
    owner = jax.vmap(lambda own, number: assign_block(jax.random.fold_in(keys[1], 2), own, number, TILES, N_DEV, 1, CAP, 2))(owner_keys, owner_turns).reshape((N_GRP, ELEMS, 1))
    target = set_ends(jax.random.randint(keys[2], (N_GRP, ELEMS), 0, ROWBLK * 5), jax.random.fold_in(keys[2], 1), 0, (ROWBLK * 5) - 1).astype(jnp.int32)
    mass = jnp.clip(jnp.exp(math.log(100.0) - 1.2039728 * jax.random.uniform(keys[3], (N_GRP, ROWS * BLK), jnp.float32) ** block_scale(keys[3], (N_GRP, ROWS * BLK), ((0, 4), (1, 8)), -0.2, 0.2)), 30.0, 100.0)
    rhs = draw_rhs(jax.random.fold_in(keys[6], 71), 0)
    faces = draw_faces(jax.random.fold_in(keys[6], 71), 0)
    return dict(tiles=tiles, owner=owner, target=target, mass=mass, rhs=rhs, faces=faces)


def assemble(tiles, owner, target):
    def one_group(args):
        group_tiles, group_owner, group_target = args
        ids = group_owner[:, 0] * (ROWBLK * 5) + group_target
        return jax.ops.segment_sum(group_tiles.astype(jnp.float32), ids, num_segments=N_DEV * ROWBLK * 5)
    return lax.map(one_group, (tiles, owner, target))


def reference(tiles, owner, target, mass, rhs, faces):
    summed = assemble(tiles, owner, target)
    blocks = summed.reshape(N_GRP, N_DEV, ROWBLK, 5, BLK, BLK)
    scale = mass.reshape(N_GRP, N_DEV, ROWBLK, BLK)
    load = rhs.reshape(N_GRP, N_DEV, ROWBLK, BLK)
    links = faces.reshape(4, N_GRP, N_DEV, ROWBLK)
    denom = scale + jnp.sum(jnp.abs(blocks), axis=(3, 5))
    colour_of = jnp.arange(ROWBLK) // COLBLK
    state = jnp.zeros((N_GRP, N_DEV, ROWBLK, BLK), jnp.float32)
    high = lax.Precision.HIGHEST
    for sweep in range(SWEEPS):
        for colour in range(COLOURS):
            padded = jnp.pad(state, ((1, 1), (1, 1), (0, 0), (0, 0)))
            sources = [padded[1:-1, :-2], padded[1:-1, 2:], padded[:-2, 1:-1], padded[2:, 1:-1]]
            seen = []
            for face in range(4):
                index = jnp.broadcast_to(links[face][..., None], state.shape)
                seen.append(jnp.take_along_axis(sources[face], index, axis=2))
            seen = jnp.stack(seen, axis=3)
            applied = jnp.einsum('gdrij,gdrj->gdri', blocks[:, :, :, 0], state, precision=high)
            applied = applied + jnp.einsum('gdrfij,gdrfj->gdri', blocks[:, :, :, 1:], seen, precision=high)
            resid = load - scale * state - applied
            chosen = (colour_of == colour)[None, None, :, None]
            state = jnp.where(chosen, state + resid / denom, state)
    return state.reshape(N_GRP, N_DEV * ROWBLK * BLK)
```

```python
import functools

import jax
import jax.numpy as jnp
from jax import lax
from jax.experimental import pallas as pl
from jax.experimental.pallas import tpu as pltpu
from jax.sharding import PartitionSpec as P

BLK = 64
COLOURS = 4
SWEEPS = 2
MESH = pl.DeviceIdType.MESH


def padded(array, sides, width):
    for axis, dim in sides:
        peers, length = (lax.axis_size(axis), array.shape[dim])
        up = [(i, (i + 1) % peers) for i in range(peers - 1)]
        down = [(j, i) for i, j in up]
        last = lax.slice_in_dim(array, length - width, length, axis=dim)
        leading = lax.slice_in_dim(array, 0, width, axis=dim)
        before = lax.ppermute(last, axis, up)
        after = lax.ppermute(leading, axis, down)
        array = jnp.concatenate([before, array, after], axis=dim)
    return array


def share(fresh):
    grid = padded(fresh.reshape(1, 1, -1), (("grp", 0), ("dev", 1)), 1)
    return jnp.stack([grid[1, 0], grid[1, 2], grid[0, 1], grid[2, 1]]).reshape(
        4, fresh.shape[0], fresh.shape[1]
    )


def pack_slots(tiles_dev, aim, where_to, peers, slots, keep):
    width = tiles_dev.shape[1]
    place = jnp.where(keep, where_to, peers * slots)
    packed = jnp.zeros((peers * slots, width), jnp.bfloat16).at[place].set(tiles_dev, mode="drop")
    labels = jnp.full((peers * slots,), -1, jnp.int32).at[place].set(aim, mode="drop")
    return (packed.reshape(peers, slots, width), labels.reshape(peers, slots))


def add_tiles(got, got_labels, slots_dev):
    width = got.shape[2]
    picks = (got_labels.reshape(1, -1) == lax.iota(jnp.int32, slots_dev)[:, None]).astype(
        jnp.bfloat16
    )
    return jnp.dot(picks, got.reshape(-1, width), preferred_element_type=jnp.float32)


def body(tiles, owner, target, mass, rhs, faces):
    count = tiles.shape[1]
    rowblk = mass.shape[1] // BLK
    colblk = rowblk // COLOURS
    peers = lax.axis_size("dev")
    slots_dev = rowblk * 5
    dest = owner[0, :, 0]
    aim = target[0]
    cap = max(2, 2 * count // peers)
    member = (dest[:, None] == lax.iota(jnp.int32, peers)[None, :]).astype(jnp.int32)
    order = jnp.sum((jnp.cumsum(member, axis=0) - 1) * member, axis=1)
    packed, labels = pack_slots(tiles[0], aim, dest * cap + order, peers, cap, order >= 0)
    got, got_labels = (
        lax.all_to_all(packed, "dev", split_axis=0, concat_axis=0, tiled=True),
        lax.all_to_all(labels, "dev", split_axis=0, concat_axis=0, tiled=True),
    )
    assembled = add_tiles(got, got_labels, slots_dev)
    blocks = assembled.reshape(rowblk, 5, BLK, BLK)
    scale = mass.reshape(rowblk, BLK)
    load = rhs.reshape(rowblk, BLK)
    links = faces[:, 0, :]
    denom = scale + jnp.sum(jnp.abs(blocks), axis=(1, 3))
    state = jnp.zeros((rowblk, BLK), jnp.float32)
    nearby = jnp.zeros((4, rowblk, BLK), jnp.float32)
    high = lax.Precision.HIGHEST
    for sweep in range(SWEEPS):
        for colour in range(COLOURS):
            low = colour * colblk
            upper = low + colblk
            seen = jnp.stack(
                [jnp.take(nearby[face], links[face, low:upper], axis=0) for face in range(4)],
                axis=1,
            )
            own = state[low:upper]
            applied = jnp.einsum("rij,rj->ri", blocks[low:upper, 0], own, precision=high)
            applied = applied + jnp.einsum(
                "rfij,rfj->ri", blocks[low:upper, 1:], seen, precision=high
            )
            resid = load[low:upper] - scale[low:upper] * own - applied
            state = state.at[low:upper].set(own + resid / denom[low:upper])
            if sweep + 1 < SWEEPS or colour + 1 < COLOURS:
                nearby = nearby.at[:, low:upper].set(share(state[low:upper]))
    return state.reshape(1, -1)

def assemble_and_smooth(pairs, cols, names, tiles_hbm, key_ref, right_ref, mass_ref, load_ref, faces_ref, out_ref,
                        tiles_v, pick_far, pick_own, far_send, far_recv, acc, line_send, up_recv, down_recv,
                        spread, mat, norm, state, near, seen, prod, fresh, face_recv,
                        tile_sem, far_ssem, far_rsem, line_ssem, up_rsem, down_rsem, fresh_ssem, face_rsem):
    grp = lax.axis_index("grp")
    dev = lax.axis_index("dev")
    n_grp, n_dev = names
    z = dev // 2
    x = dev % 2
    chunks = tiles_v.shape[0]
    slots = mat.shape[1]
    colblk = slots // (5 * COLOURS)
    near_by = [
        (dev >= 1, {"dev": dev - 1}),
        (dev < n_dev - 1, {"dev": dev + 1}),
        (grp >= 1, {"grp": grp - 1}),
        (grp < n_grp - 1, {"grp": grp + 1}),
    ]
    partners = near_by + [(dev >= 2, {"dev": dev - 2}), (dev < n_dev - 2, {"dev": dev + 2})]

    def load_tiles(k):
        return pltpu.make_async_copy(
            tiles_hbm.at[0, :, pl.ds(pl.multiple_of(k * cols, cols), cols)], tiles_v.at[k], tile_sem.at[k]
        )

    for k in range(chunks):
        load_tiles(k).start()

    barrier = pltpu.get_barrier_semaphore()
    for there, who in partners:
        @pl.when(there)
        def _():
            pl.semaphore_signal(barrier, inc=1, device_id=who, device_id_type=MESH)

    key = key_ref[...]
    right = right_ref[...]
    key_far = jnp.where(right != x, key, -1)
    key_own = jnp.where(right == x, key, -1)
    rows = lax.broadcasted_iota(jnp.int32, (slots, key.shape[1]), 0)
    for d in range(pairs):
        part = slice(d * slots, (d + 1) * slots)
        pick_far[part, :] = jnp.where(rows + d * slots == key_far, 1.0, 0.0).astype(jnp.bfloat16)

    pl.semaphore_wait(barrier, sum(there.astype(jnp.int32) for there, who in partners))

    def far_copy(k):
        return pltpu.make_async_remote_copy(
            src_ref=far_send.at[k], dst_ref=far_recv.at[k], send_sem=far_ssem.at[k], recv_sem=far_rsem.at[k],
            device_id={"dev": z * 2 + 1 - x}, device_id_type=MESH,
        )

    def up_copy(k, d):
        return pltpu.make_async_remote_copy(
            src_ref=line_send.at[k, d], dst_ref=up_recv.at[k, d], send_sem=line_ssem.at[k, d],
            recv_sem=up_rsem.at[k, d], device_id={"dev": dev + 2}, device_id_type=MESH,
        )

    def down_copy(k, d):
        return pltpu.make_async_remote_copy(
            src_ref=line_send.at[k, d], dst_ref=down_recv.at[k, d], send_sem=line_ssem.at[k, d],
            recv_sem=down_rsem.at[k, d], device_id={"dev": dev - 2}, device_id_type=MESH,
        )

    def send_far(k, carry):
        load_tiles(k).wait()
        for d in range(pairs):
            part = slice(d * slots, (d + 1) * slots)
            far_send[k, part, :] = jnp.dot(
                pick_far[part, :], tiles_v[k], preferred_element_type=jnp.float32
            ).astype(jnp.bfloat16)
        far_copy(k).start()
        return carry

    lax.fori_loop(0, chunks, send_far, 0)

    for d in range(pairs):
        part = slice(d * slots, (d + 1) * slots)
        pick_own[part, :] = jnp.where(rows + d * slots == key_own, 1.0, 0.0).astype(jnp.bfloat16)
    lane = lax.broadcasted_iota(jnp.int32, (cols, 128), 0) // BLK
    unit = lax.broadcasted_iota(jnp.int32, (cols, 128), 1) % BLK
    for k in range(chunks):
        spread[k * cols:(k + 1) * cols, :] = jnp.where(lane + k * (cols // BLK) == unit, 1.0, 0.0).astype(jnp.bfloat16)
    norm[...] = jnp.zeros_like(norm)
    near[...] = jnp.zeros_like(near)
    state[...] = jnp.zeros_like(state)

    def split(value):
        top = value.astype(jnp.bfloat16).astype(jnp.float32)
        return jnp.concatenate([top, value - top], axis=0).astype(jnp.bfloat16)

    def step(turn, carry):
        @pl.when(turn < chunks)
        def _():
            k = turn
            slot = lax.rem(k, 4)
            far_copy(k).wait_recv()
            for d in range(pairs):
                part = slice(d * slots, (d + 1) * slots)
                acc[slot, d] = jnp.dot(
                    pick_own[part, :], tiles_v[k], preferred_element_type=jnp.float32
                ) + far_recv[k, part, :].astype(jnp.float32)
            for d in reversed(range(1, pairs)):
                @pl.when(z == 0)
                def _():
                    line_send[k, d] = acc[slot, d].astype(jnp.bfloat16)
                    up_copy(k, d).start()
            for d in range(pairs - 1):
                @pl.when(z == pairs - 1)
                def _():
                    line_send[k, d] = acc[slot, d].astype(jnp.bfloat16)
                    down_copy(k, d).start()

        @pl.when((turn >= 1) & (turn < chunks + 1))
        def _():
            k = turn - 1
            slot = lax.rem(k, 4)
            for e in range(1, pairs):
                d = pairs - e
                @pl.when((z > 0) & (z < d))
                def _():
                    up_copy(k, d).wait_recv()
                    line_send[k, d] = (acc[slot, d] + up_recv[k, d].astype(jnp.float32)).astype(jnp.bfloat16)
                    up_copy(k, d).start()
                g = e - 1
                @pl.when((z < pairs - 1) & (z > g))
                def _():
                    down_copy(k, g).wait_recv()
                    line_send[k, g] = (acc[slot, g] + down_recv[k, g].astype(jnp.float32)).astype(jnp.bfloat16)
                    down_copy(k, g).start()

        @pl.when(turn >= 2)
        def _():
            k = turn - 2
            slot = lax.rem(k, 4)
            mat[k] = acc[slot, z]

            @pl.when(z > 0)
            def _():
                up_copy(k, z).wait_recv()
                mat[k] = mat[k] + up_recv[k, z].astype(jnp.float32)

            @pl.when(z < pairs - 1)
            def _():
                down_copy(k, z).wait_recv()
                mat[k] = mat[k] + down_recv[k, z].astype(jnp.float32)

            size = jnp.abs(mat[k]).reshape(COLOURS, 5, colblk, cols)
            size = jnp.sum(size, axis=1).reshape(COLOURS * colblk, cols)
            norm[...] += jnp.dot(
                split(size), spread[pl.ds(pl.multiple_of(k * cols, cols), cols), :],
                preferred_element_type=jnp.float32,
            )

        return carry

    lax.fori_loop(0, chunks + 2, step, 0)

    half = COLOURS * colblk
    norm[:half, :] = 1.0 / (mass_ref[...] + norm[:half, :] + norm[half:, :])

    def fresh_copy(turn, face):
        return pltpu.make_async_remote_copy(
            src_ref=fresh.at[turn], dst_ref=face_recv.at[turn, face ^ 1], send_sem=fresh_ssem.at[turn, face],
            recv_sem=face_rsem.at[turn, face ^ 1], device_id=near_by[face][1], device_id_type=MESH,
        )

    def face_wait(turn, face):
        pltpu.make_async_remote_copy(
            src_ref=fresh.at[turn], dst_ref=face_recv.at[turn, face], send_sem=fresh_ssem.at[turn, face],
            recv_sem=face_rsem.at[turn, face], device_id=near_by[face][1], device_id_type=MESH,
        ).wait_recv()

    last = SWEEPS * COLOURS - 1
    for turn in range(last + 1):
        colour = turn % COLOURS
        low = colour * colblk
        part = slice(low, low + colblk)
        own = state[part, :]
        resid = load_ref[part, :] - mass_ref[part, :] * own
        if turn > 0:
            for face in range(4):
                for r in range(colblk):
                    seen[face, r:r + 1, :] = near[face, pl.ds(faces_ref[face, low + r], 1), :]
            sides = [own] + [seen[face] for face in range(4)]
            for k in range(chunks):
                for h in range(cols // 128):
                    total = None
                    for s in range(5):
                        at = (colour * 5 + s) * colblk
                        term = mat[k, at:at + colblk, h * 128:(h + 1) * 128] * sides[s]
                        total = term if total is None else total + term
                    at = k * cols + h * 128
                    prod[:, at:at + 128] = split(total)
            applied = jnp.dot(prod[...], spread[...], preferred_element_type=jnp.float32)
            resid = resid - (applied[:colblk] + applied[colblk:])
        value = own + resid * norm[part, :]
        state[part, :] = value
        if turn < last:
            fresh[turn] = value
            for face in range(4):
                @pl.when(near_by[face][0])
                def _():
                    fresh_copy(turn, face).start()
            for face in range(4):
                @pl.when(near_by[face][0])
                def _():
                    face_wait(turn, face)
                    near[face, part, :] = face_recv[turn, face]
    out_ref[...] = state[...]

    for turn in range(last):
        for face in range(4):
            @pl.when(near_by[face][0])
            def _():
                fresh_copy(turn, face).wait_send()

    def drain(k, carry):
        far_copy(k).wait_send()
        for d in range(pairs):
            @pl.when(z < d)
            def _():
                up_copy(k, d).wait_send()

            @pl.when(z > d)
            def _():
                down_copy(k, d).wait_send()
        return carry

    lax.fori_loop(0, chunks, drain, 0)


def fused(tiles, owner, target, mass, rhs, faces):
    count, width = tiles.shape[1:]
    rowblk = mass.shape[1] // BLK
    colblk = rowblk // COLOURS
    peers = lax.axis_size("dev")
    pairs = peers // 2
    slots = rowblk * 5
    cols = 256
    chunks = width // cols
    dest = owner.reshape(1, count)
    row, side = target // 5, target % 5
    place = ((row // colblk) * 5 + side) * colblk + row % colblk
    key = (dest // 2) * slots + place
    right = dest % 2

    def twice(value):
        value = value.reshape(rowblk, BLK)
        return jnp.concatenate([value, value], axis=1)

    vmem = pl.BlockSpec(memory_space=pltpu.VMEM)
    steps = SWEEPS * COLOURS - 1
    out = pl.pallas_call(
        functools.partial(assemble_and_smooth, pairs, cols, (lax.axis_size("grp"), peers)),
        out_shape=jax.ShapeDtypeStruct((rowblk, 2 * BLK), jnp.float32),
        in_specs=[pl.BlockSpec(memory_space=pl.ANY), vmem, vmem, vmem, vmem, pl.BlockSpec(memory_space=pltpu.SMEM)],
        out_specs=vmem,
        scratch_shapes=[
            pltpu.VMEM((chunks, count, cols), jnp.bfloat16),
            pltpu.VMEM((pairs * slots, count), jnp.bfloat16),
            pltpu.VMEM((pairs * slots, count), jnp.bfloat16),
            pltpu.VMEM((chunks, pairs * slots, cols), jnp.bfloat16),
            pltpu.VMEM((chunks, pairs * slots, cols), jnp.bfloat16),
            pltpu.VMEM((4, pairs, slots, cols), jnp.float32),
            pltpu.VMEM((chunks, pairs, slots, cols), jnp.bfloat16),
            pltpu.VMEM((chunks, pairs, slots, cols), jnp.bfloat16),
            pltpu.VMEM((chunks, pairs, slots, cols), jnp.bfloat16),
            pltpu.VMEM((width, 2 * BLK), jnp.bfloat16),
            pltpu.VMEM((chunks, slots, cols), jnp.float32),
            pltpu.VMEM((2 * rowblk, 2 * BLK), jnp.float32),
            pltpu.VMEM((rowblk, 2 * BLK), jnp.float32),
            pltpu.VMEM((4, rowblk, 2 * BLK), jnp.float32),
            pltpu.VMEM((4, colblk, 2 * BLK), jnp.float32),
            pltpu.VMEM((2 * colblk, width), jnp.bfloat16),
            pltpu.VMEM((steps, colblk, 2 * BLK), jnp.float32),
            pltpu.VMEM((steps, 4, colblk, 2 * BLK), jnp.float32),
            pltpu.SemaphoreType.DMA((chunks,)),
            pltpu.SemaphoreType.DMA((chunks,)),
            pltpu.SemaphoreType.DMA((chunks,)),
            pltpu.SemaphoreType.DMA((chunks, pairs)),
            pltpu.SemaphoreType.DMA((chunks, pairs)),
            pltpu.SemaphoreType.DMA((chunks, pairs)),
            pltpu.SemaphoreType.DMA((steps, 4)),
            pltpu.SemaphoreType.DMA((steps, 4)),
        ],
        compiler_params=pltpu.CompilerParams(
            collective_id=0, has_side_effects=True, vmem_limit_bytes=58 * 1024 * 1024
        ),
    )(tiles, key, right, twice(mass), twice(rhs), faces[:, 0, :])
    return out[:, :BLK].reshape(1, -1)


def solution(mesh):
    placed = (
        P("grp", "dev", None),
        P("grp", "dev", None),
        P("grp", "dev"),
        P("grp", "dev"),
        P("grp", "dev"),
        P(None, "grp", "dev"),
    )
    peers = mesh.shape["dev"]
    return jax.shard_map(
        fused if peers % 2 == 0 and peers <= 8 else body,
        mesh=mesh, in_specs=placed, out_specs=P("grp", "dev"), check_vma=False,
    )
```

```python
import functools

import jax
import jax.numpy as jnp
from jax import lax
from jax.experimental import pallas as pl
from jax.experimental.pallas import tpu as pltpu
from jax.sharding import PartitionSpec as P

BLK = 64
COLOURS = 4
SWEEPS = 2
MESH = pl.DeviceIdType.MESH


def padded(array, sides, width):
    for axis, dim in sides:
        peers, length = (lax.axis_size(axis), array.shape[dim])
        up = [(i, (i + 1) % peers) for i in range(peers - 1)]
        down = [(j, i) for i, j in up]
        last = lax.slice_in_dim(array, length - width, length, axis=dim)
        leading = lax.slice_in_dim(array, 0, width, axis=dim)
        before = lax.ppermute(last, axis, up)
        after = lax.ppermute(leading, axis, down)
        array = jnp.concatenate([before, array, after], axis=dim)
    return array


def share(fresh):
    grid = padded(fresh.reshape(1, 1, -1), (("grp", 0), ("dev", 1)), 1)
    return jnp.stack([grid[1, 0], grid[1, 2], grid[0, 1], grid[2, 1]]).reshape(
        4, fresh.shape[0], fresh.shape[1]
    )


def pack_slots(tiles_dev, aim, where_to, peers, slots, keep):
    width = tiles_dev.shape[1]
    place = jnp.where(keep, where_to, peers * slots)
    packed = jnp.zeros((peers * slots, width), jnp.bfloat16).at[place].set(tiles_dev, mode="drop")
    labels = jnp.full((peers * slots,), -1, jnp.int32).at[place].set(aim, mode="drop")
    return (packed.reshape(peers, slots, width), labels.reshape(peers, slots))


def add_tiles(got, got_labels, slots_dev):
    width = got.shape[2]
    picks = (got_labels.reshape(1, -1) == lax.iota(jnp.int32, slots_dev)[:, None]).astype(
        jnp.bfloat16
    )
    return jnp.dot(picks, got.reshape(-1, width), preferred_element_type=jnp.float32)


def body(tiles, owner, target, mass, rhs, faces):
    count = tiles.shape[1]
    rowblk = mass.shape[1] // BLK
    colblk = rowblk // COLOURS
    peers = lax.axis_size("dev")
    slots_dev = rowblk * 5
    dest = owner[0, :, 0]
    aim = target[0]
    cap = max(2, 2 * count // peers)
    member = (dest[:, None] == lax.iota(jnp.int32, peers)[None, :]).astype(jnp.int32)
    order = jnp.sum((jnp.cumsum(member, axis=0) - 1) * member, axis=1)
    packed, labels = pack_slots(tiles[0], aim, dest * cap + order, peers, cap, order >= 0)
    got, got_labels = (
        lax.all_to_all(packed, "dev", split_axis=0, concat_axis=0, tiled=True),
        lax.all_to_all(labels, "dev", split_axis=0, concat_axis=0, tiled=True),
    )
    assembled = add_tiles(got, got_labels, slots_dev)
    blocks = assembled.reshape(rowblk, 5, BLK, BLK)
    scale = mass.reshape(rowblk, BLK)
    load = rhs.reshape(rowblk, BLK)
    links = faces[:, 0, :]
    denom = scale + jnp.sum(jnp.abs(blocks), axis=(1, 3))
    state = jnp.zeros((rowblk, BLK), jnp.float32)
    nearby = jnp.zeros((4, rowblk, BLK), jnp.float32)
    high = lax.Precision.HIGHEST
    for sweep in range(SWEEPS):
        for colour in range(COLOURS):
            low = colour * colblk
            upper = low + colblk
            seen = jnp.stack(
                [jnp.take(nearby[face], links[face, low:upper], axis=0) for face in range(4)],
                axis=1,
            )
            own = state[low:upper]
            applied = jnp.einsum("rij,rj->ri", blocks[low:upper, 0], own, precision=high)
            applied = applied + jnp.einsum(
                "rfij,rfj->ri", blocks[low:upper, 1:], seen, precision=high
            )
            resid = load[low:upper] - scale[low:upper] * own - applied
            state = state.at[low:upper].set(own + resid / denom[low:upper])
            if sweep + 1 < SWEEPS or colour + 1 < COLOURS:
                nearby = nearby.at[:, low:upper].set(share(state[low:upper]))
    return state.reshape(1, -1)

def assemble_and_smooth(pairs, cols, names, tiles_hbm, key_ref, right_ref, mass_ref, load_ref, faces_ref, out_ref,
                        tiles_v, pick_far, pick_own, far_send, far_recv, acc, line_send, up_recv, down_recv,
                        spread, mat, norm, state, near, seen, prod, fresh, face_recv,
                        tile_sem, far_ssem, far_rsem, line_ssem, up_rsem, down_rsem, fresh_ssem, face_rsem):
    grp = lax.axis_index("grp")
    dev = lax.axis_index("dev")
    n_grp, n_dev = names
    z = dev // 2
    x = dev % 2
    chunks = tiles_v.shape[0]
    slots = mat.shape[1]
    colblk = slots // (5 * COLOURS)
    near_by = [
        (dev >= 1, {"dev": dev - 1}),
        (dev < n_dev - 1, {"dev": dev + 1}),
        (grp >= 1, {"grp": grp - 1}),
        (grp < n_grp - 1, {"grp": grp + 1}),
    ]
    partners = near_by + [(dev >= 2, {"dev": dev - 2}), (dev < n_dev - 2, {"dev": dev + 2})]

    def load_tiles(k):
        return pltpu.make_async_copy(
            tiles_hbm.at[0, :, pl.ds(pl.multiple_of(k * cols, cols), cols)], tiles_v.at[k], tile_sem.at[k]
        )

    for k in range(chunks):
        load_tiles(k).start()

    barrier = pltpu.get_barrier_semaphore()
    for there, who in partners:
        @pl.when(there)
        def _():
            pl.semaphore_signal(barrier, inc=1, device_id=who, device_id_type=MESH)

    key = key_ref[...]
    right = right_ref[...]
    key_far = jnp.where(right != x, key, -1)
    key_own = jnp.where(right == x, key, -1)
    rows = lax.broadcasted_iota(jnp.int32, (slots, key.shape[1]), 0)
    for d in range(pairs):
        part = slice(d * slots, (d + 1) * slots)
        pick_far[part, :] = jnp.where(rows + d * slots == key_far, 1.0, 0.0).astype(jnp.bfloat16)

    pl.semaphore_wait(barrier, sum(there.astype(jnp.int32) for there, who in partners))

    def far_copy(k):
        return pltpu.make_async_remote_copy(
            src_ref=far_send.at[k], dst_ref=far_recv.at[k], send_sem=far_ssem.at[k], recv_sem=far_rsem.at[k],
            device_id={"dev": z * 2 + 1 - x}, device_id_type=MESH,
        )

    def up_copy(k, d):
        return pltpu.make_async_remote_copy(
            src_ref=line_send.at[k, d], dst_ref=up_recv.at[k, d], send_sem=line_ssem.at[k, d],
            recv_sem=up_rsem.at[k, d], device_id={"dev": dev + 2}, device_id_type=MESH,
        )

    def down_copy(k, d):
        return pltpu.make_async_remote_copy(
            src_ref=line_send.at[k, d], dst_ref=down_recv.at[k, d], send_sem=line_ssem.at[k, d],
            recv_sem=down_rsem.at[k, d], device_id={"dev": dev - 2}, device_id_type=MESH,
        )

    def send_far(k, carry):
        load_tiles(k).wait()
        for d in range(pairs):
            part = slice(d * slots, (d + 1) * slots)
            far_send[k, part, :] = jnp.dot(
                pick_far[part, :], tiles_v[k], preferred_element_type=jnp.float32
            ).astype(jnp.bfloat16)
        far_copy(k).start()
        return carry

    lax.fori_loop(0, chunks, send_far, 0)

    for d in range(pairs):
        part = slice(d * slots, (d + 1) * slots)
        pick_own[part, :] = jnp.where(rows + d * slots == key_own, 1.0, 0.0).astype(jnp.bfloat16)
    lane = lax.broadcasted_iota(jnp.int32, (cols, 128), 0) // BLK
    unit = lax.broadcasted_iota(jnp.int32, (cols, 128), 1) % BLK
    for k in range(chunks):
        spread[k * cols:(k + 1) * cols, :] = jnp.where(lane + k * (cols // BLK) == unit, 1.0, 0.0).astype(jnp.bfloat16)
    norm[...] = jnp.zeros_like(norm)
    near[...] = jnp.zeros_like(near)
    state[...] = jnp.zeros_like(state)

    def split(value):
        top = value.astype(jnp.bfloat16).astype(jnp.float32)
        return jnp.concatenate([top, value - top], axis=0).astype(jnp.bfloat16)

    def step(turn, carry):
        @pl.when(turn < chunks)
        def _():
            k = turn
            slot = lax.rem(k, pairs)
            far_copy(k).wait_recv()
            for d in range(pairs):
                part = slice(d * slots, (d + 1) * slots)
                acc[slot, d] = jnp.dot(
                    pick_own[part, :], tiles_v[k], preferred_element_type=jnp.float32
                ) + far_recv[k, part, :].astype(jnp.float32)
            for d in reversed(range(1, pairs)):
                @pl.when(z == 0)
                def _():
                    line_send[k, d] = acc[slot, d].astype(jnp.bfloat16)
                    up_copy(k, d).start()
            for d in range(pairs - 1):
                @pl.when(z == pairs - 1)
                def _():
                    line_send[k, d] = acc[slot, d].astype(jnp.bfloat16)
                    down_copy(k, d).start()

        down_lag = pairs - 1 - z
        for e in range(1, pairs):
            d = pairs - e
            @pl.when((z > 0) & (z < d) & (turn >= z) & (turn < chunks + z))
            def _():
                k = turn - z
                slot = lax.rem(k, pairs)
                up_copy(k, d).wait_recv()
                line_send[k, d] = (acc[slot, d] + up_recv[k, d].astype(jnp.float32)).astype(jnp.bfloat16)
                up_copy(k, d).start()
            g = e - 1
            @pl.when((z < pairs - 1) & (z > g) & (turn >= down_lag) & (turn < chunks + down_lag))
            def _():
                k = turn - down_lag
                slot = lax.rem(k, pairs)
                down_copy(k, g).wait_recv()
                line_send[k, g] = (acc[slot, g] + down_recv[k, g].astype(jnp.float32)).astype(jnp.bfloat16)
                down_copy(k, g).start()

        @pl.when(turn >= pairs - 1)
        def _():
            k = turn - (pairs - 1)
            slot = lax.rem(k, pairs)
            mat[k] = acc[slot, z]

            @pl.when(z > 0)
            def _():
                up_copy(k, z).wait_recv()
                mat[k] = mat[k] + up_recv[k, z].astype(jnp.float32)

            @pl.when(z < pairs - 1)
            def _():
                down_copy(k, z).wait_recv()
                mat[k] = mat[k] + down_recv[k, z].astype(jnp.float32)

            size = jnp.abs(mat[k]).reshape(COLOURS, 5, colblk, cols)
            size = jnp.sum(size, axis=1).reshape(COLOURS * colblk, cols)
            norm[...] += jnp.dot(
                split(size), spread[pl.ds(pl.multiple_of(k * cols, cols), cols), :],
                preferred_element_type=jnp.float32,
            )

        return carry

    lax.fori_loop(0, chunks + pairs - 1, step, 0)

    half = COLOURS * colblk
    norm[:half, :] = 1.0 / (mass_ref[...] + norm[:half, :] + norm[half:, :])

    def fresh_copy(turn, face):
        return pltpu.make_async_remote_copy(
            src_ref=fresh.at[turn], dst_ref=face_recv.at[turn, face ^ 1], send_sem=fresh_ssem.at[turn, face],
            recv_sem=face_rsem.at[turn, face ^ 1], device_id=near_by[face][1], device_id_type=MESH,
        )

    def face_wait(turn, face):
        pltpu.make_async_remote_copy(
            src_ref=fresh.at[turn], dst_ref=face_recv.at[turn, face], send_sem=fresh_ssem.at[turn, face],
            recv_sem=face_rsem.at[turn, face], device_id=near_by[face][1], device_id_type=MESH,
        ).wait_recv()

    last = SWEEPS * COLOURS - 1
    for turn in range(last + 1):
        colour = turn % COLOURS
        low = colour * colblk
        part = slice(low, low + colblk)
        own = state[part, :]
        resid = load_ref[part, :] - mass_ref[part, :] * own
        if turn > 0:
            for face in range(4):
                for r in range(colblk):
                    seen[face, r:r + 1, :] = near[face, pl.ds(faces_ref[face, low + r], 1), :]
            sides = [own] + [seen[face] for face in range(4)]
            for k in range(chunks):
                for h in range(cols // 128):
                    total = None
                    for s in range(5):
                        at = (colour * 5 + s) * colblk
                        term = mat[k, at:at + colblk, h * 128:(h + 1) * 128] * sides[s]
                        total = term if total is None else total + term
                    at = k * cols + h * 128
                    prod[:, at:at + 128] = split(total)
            applied = jnp.dot(prod[...], spread[...], preferred_element_type=jnp.float32)
            resid = resid - (applied[:colblk] + applied[colblk:])
        value = own + resid * norm[part, :]
        state[part, :] = value
        if turn < last:
            fresh[turn] = value
            for face in range(4):
                @pl.when(near_by[face][0])
                def _():
                    fresh_copy(turn, face).start()
            for face in range(4):
                @pl.when(near_by[face][0])
                def _():
                    face_wait(turn, face)
                    near[face, part, :] = face_recv[turn, face]
    out_ref[...] = state[...]

    for turn in range(last):
        for face in range(4):
            @pl.when(near_by[face][0])
            def _():
                fresh_copy(turn, face).wait_send()

    def drain(k, carry):
        far_copy(k).wait_send()
        for d in range(pairs):
            @pl.when(z < d)
            def _():
                up_copy(k, d).wait_send()

            @pl.when(z > d)
            def _():
                down_copy(k, d).wait_send()
        return carry

    lax.fori_loop(0, chunks, drain, 0)


def fused(tiles, owner, target, mass, rhs, faces):
    count, width = tiles.shape[1:]
    rowblk = mass.shape[1] // BLK
    colblk = rowblk // COLOURS
    peers = lax.axis_size("dev")
    pairs = peers // 2
    slots = rowblk * 5
    cols = 256
    chunks = width // cols
    dest = owner.reshape(1, count)
    row, side = target // 5, target % 5
    place = ((row // colblk) * 5 + side) * colblk + row % colblk
    key = (dest // 2) * slots + place
    right = dest % 2

    def twice(value):
        value = value.reshape(rowblk, BLK)
        return jnp.concatenate([value, value], axis=1)

    vmem = pl.BlockSpec(memory_space=pltpu.VMEM)
    steps = SWEEPS * COLOURS - 1
    out = pl.pallas_call(
        functools.partial(assemble_and_smooth, pairs, cols, (lax.axis_size("grp"), peers)),
        out_shape=jax.ShapeDtypeStruct((rowblk, 2 * BLK), jnp.float32),
        in_specs=[pl.BlockSpec(memory_space=pl.ANY), vmem, vmem, vmem, vmem, pl.BlockSpec(memory_space=pltpu.SMEM)],
        out_specs=vmem,
        scratch_shapes=[
            pltpu.VMEM((chunks, count, cols), jnp.bfloat16),
            pltpu.VMEM((pairs * slots, count), jnp.bfloat16),
            pltpu.VMEM((pairs * slots, count), jnp.bfloat16),
            pltpu.VMEM((chunks, pairs * slots, cols), jnp.bfloat16),
            pltpu.VMEM((chunks, pairs * slots, cols), jnp.bfloat16),
            pltpu.VMEM((pairs, pairs, slots, cols), jnp.float32),
            pltpu.VMEM((chunks, pairs, slots, cols), jnp.bfloat16),
            pltpu.VMEM((chunks, pairs, slots, cols), jnp.bfloat16),
            pltpu.VMEM((chunks, pairs, slots, cols), jnp.bfloat16),
            pltpu.VMEM((width, 2 * BLK), jnp.bfloat16),
            pltpu.VMEM((chunks, slots, cols), jnp.float32),
            pltpu.VMEM((2 * rowblk, 2 * BLK), jnp.float32),
            pltpu.VMEM((rowblk, 2 * BLK), jnp.float32),
            pltpu.VMEM((4, rowblk, 2 * BLK), jnp.float32),
            pltpu.VMEM((4, colblk, 2 * BLK), jnp.float32),
            pltpu.VMEM((2 * colblk, width), jnp.bfloat16),
            pltpu.VMEM((steps, colblk, 2 * BLK), jnp.float32),
            pltpu.VMEM((steps, 4, colblk, 2 * BLK), jnp.float32),
            pltpu.SemaphoreType.DMA((chunks,)),
            pltpu.SemaphoreType.DMA((chunks,)),
            pltpu.SemaphoreType.DMA((chunks,)),
            pltpu.SemaphoreType.DMA((chunks, pairs)),
            pltpu.SemaphoreType.DMA((chunks, pairs)),
            pltpu.SemaphoreType.DMA((chunks, pairs)),
            pltpu.SemaphoreType.DMA((steps, 4)),
            pltpu.SemaphoreType.DMA((steps, 4)),
        ],
        compiler_params=pltpu.CompilerParams(
            collective_id=0, has_side_effects=True, vmem_limit_bytes=58 * 1024 * 1024
        ),
    )(tiles, key, right, twice(mass), twice(rhs), faces[:, 0, :])
    return out[:, :BLK].reshape(1, -1)


def solution(mesh):
    placed = (
        P("grp", "dev", None),
        P("grp", "dev", None),
        P("grp", "dev"),
        P("grp", "dev"),
        P("grp", "dev"),
        P(None, "grp", "dev"),
    )
    peers = mesh.shape["dev"]
    return jax.shard_map(
        fused if peers % 2 == 0 and peers <= 8 else body,
        mesh=mesh, in_specs=placed, out_specs=P("grp", "dev"), check_vma=False,
    )
```

```python
import functools

import jax
import jax.numpy as jnp
from jax import lax
from jax.experimental import pallas as pl
from jax.experimental.pallas import tpu as pltpu
from jax.sharding import PartitionSpec as P

BLK = 64
COLOURS = 4
SWEEPS = 2
MESH = pl.DeviceIdType.MESH


def padded(array, sides, width):
    for axis, dim in sides:
        peers, length = (lax.axis_size(axis), array.shape[dim])
        up = [(i, (i + 1) % peers) for i in range(peers - 1)]
        down = [(j, i) for i, j in up]
        last = lax.slice_in_dim(array, length - width, length, axis=dim)
        leading = lax.slice_in_dim(array, 0, width, axis=dim)
        before = lax.ppermute(last, axis, up)
        after = lax.ppermute(leading, axis, down)
        array = jnp.concatenate([before, array, after], axis=dim)
    return array


def share(fresh):
    grid = padded(fresh.reshape(1, 1, -1), (("grp", 0), ("dev", 1)), 1)
    return jnp.stack([grid[1, 0], grid[1, 2], grid[0, 1], grid[2, 1]]).reshape(
        4, fresh.shape[0], fresh.shape[1]
    )


def pack_slots(tiles_dev, aim, where_to, peers, slots, keep):
    width = tiles_dev.shape[1]
    place = jnp.where(keep, where_to, peers * slots)
    packed = jnp.zeros((peers * slots, width), jnp.bfloat16).at[place].set(tiles_dev, mode="drop")
    labels = jnp.full((peers * slots,), -1, jnp.int32).at[place].set(aim, mode="drop")
    return (packed.reshape(peers, slots, width), labels.reshape(peers, slots))


def add_tiles(got, got_labels, slots_dev):
    width = got.shape[2]
    picks = (got_labels.reshape(1, -1) == lax.iota(jnp.int32, slots_dev)[:, None]).astype(
        jnp.bfloat16
    )
    return jnp.dot(picks, got.reshape(-1, width), preferred_element_type=jnp.float32)


def body(tiles, owner, target, mass, rhs, faces):
    count = tiles.shape[1]
    rowblk = mass.shape[1] // BLK
    colblk = rowblk // COLOURS
    peers = lax.axis_size("dev")
    slots_dev = rowblk * 5
    dest = owner[0, :, 0]
    aim = target[0]
    cap = max(2, 2 * count // peers)
    member = (dest[:, None] == lax.iota(jnp.int32, peers)[None, :]).astype(jnp.int32)
    order = jnp.sum((jnp.cumsum(member, axis=0) - 1) * member, axis=1)
    packed, labels = pack_slots(tiles[0], aim, dest * cap + order, peers, cap, order >= 0)
    got, got_labels = (
        lax.all_to_all(packed, "dev", split_axis=0, concat_axis=0, tiled=True),
        lax.all_to_all(labels, "dev", split_axis=0, concat_axis=0, tiled=True),
    )
    assembled = add_tiles(got, got_labels, slots_dev)
    blocks = assembled.reshape(rowblk, 5, BLK, BLK)
    scale = mass.reshape(rowblk, BLK)
    load = rhs.reshape(rowblk, BLK)
    links = faces[:, 0, :]
    denom = scale + jnp.sum(jnp.abs(blocks), axis=(1, 3))
    state = jnp.zeros((rowblk, BLK), jnp.float32)
    nearby = jnp.zeros((4, rowblk, BLK), jnp.float32)
    high = lax.Precision.HIGHEST
    for sweep in range(SWEEPS):
        for colour in range(COLOURS):
            low = colour * colblk
            upper = low + colblk
            seen = jnp.stack(
                [jnp.take(nearby[face], links[face, low:upper], axis=0) for face in range(4)],
                axis=1,
            )
            own = state[low:upper]
            applied = jnp.einsum("rij,rj->ri", blocks[low:upper, 0], own, precision=high)
            applied = applied + jnp.einsum(
                "rfij,rfj->ri", blocks[low:upper, 1:], seen, precision=high
            )
            resid = load[low:upper] - scale[low:upper] * own - applied
            state = state.at[low:upper].set(own + resid / denom[low:upper])
            if sweep + 1 < SWEEPS or colour + 1 < COLOURS:
                nearby = nearby.at[:, low:upper].set(share(state[low:upper]))
    return state.reshape(1, -1)

def assemble_and_smooth(pairs, cols, early, names, tiles_hbm, key_ref, right_ref, mass_ref, load_ref, faces_ref, out_ref,
                        tiles_v, pick_far, pick_own, far_send, far_recv, acc, line_send, up_recv, down_recv, pair_send, pair_recv,
                        spread, mat, norm, state, near, seen, prod, fresh, face_recv,
                        tile_sem, far_ssem, far_rsem, line_ssem, up_rsem, down_rsem, fresh_ssem, face_rsem, pair_ssem, pair_rsem):
    grp = lax.axis_index("grp")
    dev = lax.axis_index("dev")
    n_grp, n_dev = names
    z = dev // 2
    x = dev % 2
    chunks = tiles_v.shape[0]
    lines = chunks + early
    slots = mat.shape[1]
    colblk = slots // (5 * COLOURS)
    near_by = [
        (dev >= 1, {"dev": dev - 1}),
        (dev < n_dev - 1, {"dev": dev + 1}),
        (grp >= 1, {"grp": grp - 1}),
        (grp < n_grp - 1, {"grp": grp + 1}),
    ]
    partners = near_by + [(dev >= 2, {"dev": dev - 2}), (dev < n_dev - 2, {"dev": dev + 2})]

    def load_tiles(k):
        return pltpu.make_async_copy(
            tiles_hbm.at[0, :, pl.ds(pl.multiple_of(k * cols, cols), cols)], tiles_v.at[k], tile_sem.at[k]
        )

    for k in range(chunks):
        load_tiles(k).start()

    barrier = pltpu.get_barrier_semaphore()
    for there, who in partners:
        @pl.when(there)
        def _():
            pl.semaphore_signal(barrier, inc=1, device_id=who, device_id_type=MESH)

    key = key_ref[...]
    right = right_ref[...]
    key_far = jnp.where(right != x, key, -1)
    key_own = jnp.where(right == x, key, -1)
    rows = lax.broadcasted_iota(jnp.int32, (slots, key.shape[1]), 0)
    for d in range(pairs):
        part = slice(d * slots, (d + 1) * slots)
        pick_far[part, :] = jnp.where(rows + d * slots == key_far, 1.0, 0.0).astype(jnp.bfloat16)

    pl.semaphore_wait(barrier, sum(there.astype(jnp.int32) for there, who in partners))

    def far_copy(k):
        return pltpu.make_async_remote_copy(
            src_ref=far_send.at[k], dst_ref=far_recv.at[k], send_sem=far_ssem.at[k], recv_sem=far_rsem.at[k],
            device_id={"dev": z * 2 + 1 - x}, device_id_type=MESH,
        )

    def pair_copy(c):
        return pltpu.make_async_remote_copy(
            src_ref=pair_send.at[c], dst_ref=pair_recv.at[c], send_sem=pair_ssem.at[c], recv_sem=pair_rsem.at[c],
            device_id={"dev": z * 2 + 1 - x}, device_id_type=MESH,
        )

    def up_copy(k, d):
        return pltpu.make_async_remote_copy(
            src_ref=line_send.at[k, d], dst_ref=up_recv.at[k, d], send_sem=line_ssem.at[k, d],
            recv_sem=up_rsem.at[k, d], device_id={"dev": dev + 2}, device_id_type=MESH,
        )

    def down_copy(k, d):
        return pltpu.make_async_remote_copy(
            src_ref=line_send.at[k, d], dst_ref=down_recv.at[k, d], send_sem=line_ssem.at[k, d],
            recv_sem=down_rsem.at[k, d], device_id={"dev": dev - 2}, device_id_type=MESH,
        )

    def send_far(k, carry):
        load_tiles(k).wait()
        for d in range(pairs):
            part = slice(d * slots, (d + 1) * slots)
            far_send[k, part, :] = jnp.dot(
                pick_far[part, :], tiles_v[k], preferred_element_type=jnp.float32
            ).astype(jnp.bfloat16)
        far_copy(k).start()
        return carry

    for c in range(early):
        load_tiles(c).wait()
    lax.fori_loop(early, chunks, send_far, 0)

    for d in range(pairs):
        part = slice(d * slots, (d + 1) * slots)
        pick_own[part, :] = jnp.where(rows + d * slots == key_own, 1.0, 0.0).astype(jnp.bfloat16)
    lane = lax.broadcasted_iota(jnp.int32, (cols, 128), 0) // BLK
    unit = lax.broadcasted_iota(jnp.int32, (cols, 128), 1) % BLK
    for k in range(chunks):
        spread[k * cols:(k + 1) * cols, :] = jnp.where(lane + k * (cols // BLK) == unit, 1.0, 0.0).astype(jnp.bfloat16)
    norm[...] = jnp.zeros_like(norm)
    near[...] = jnp.zeros_like(near)
    state[...] = jnp.zeros_like(state)

    def split(value):
        top = value.astype(jnp.bfloat16).astype(jnp.float32)
        return jnp.concatenate([top, value - top], axis=0).astype(jnp.bfloat16)

    def finish(v, k, slot):
        mat[k] = acc[slot, z]

        @pl.when(z > 0)
        def _():
            up_copy(v, z).wait_recv()
            mat[k] = mat[k] + up_recv[v, z].astype(jnp.float32)

        @pl.when(z < pairs - 1)
        def _():
            down_copy(v, z).wait_recv()
            mat[k] = mat[k] + down_recv[v, z].astype(jnp.float32)

    def add_norm(k):
        size = jnp.abs(mat[k]).reshape(COLOURS, 5, colblk, cols)
        size = jnp.sum(size, axis=1).reshape(COLOURS * colblk, cols)
        at = k * cols if isinstance(k, int) else pl.multiple_of(k * cols, cols)
        norm[...] += jnp.dot(split(size), spread[pl.ds(at, cols), :], preferred_element_type=jnp.float32)

    def step(turn, carry):
        for v in range(2 * early):
            @pl.when(turn == v)
            def _():
                pick = pick_own if v % 2 else pick_far
                for d in range(pairs):
                    acc[v % pairs, d] = jnp.dot(
                        pick[d * slots:(d + 1) * slots, :], tiles_v[v // 2], preferred_element_type=jnp.float32
                    )

        @pl.when((turn >= 2 * early) & (turn < lines))
        def _():
            k = turn - early
            slot = lax.rem(turn, pairs)
            far_copy(k).wait_recv()
            for d in range(pairs):
                part = slice(d * slots, (d + 1) * slots)
                acc[slot, d] = jnp.dot(
                    pick_own[part, :], tiles_v[k], preferred_element_type=jnp.float32
                ) + far_recv[k, part, :].astype(jnp.float32)

        @pl.when(turn < lines)
        def _():
            k = turn
            slot = lax.rem(k, pairs)
            for d in reversed(range(1, pairs)):
                @pl.when(z == 0)
                def _():
                    line_send[k, d] = acc[slot, d].astype(jnp.bfloat16)
                    up_copy(k, d).start()
            for d in range(pairs - 1):
                @pl.when(z == pairs - 1)
                def _():
                    line_send[k, d] = acc[slot, d].astype(jnp.bfloat16)
                    down_copy(k, d).start()

        down_lag = pairs - 1 - z
        for e in range(1, pairs):
            d = pairs - e
            @pl.when((z > 0) & (z < d) & (turn >= z) & (turn < lines + z))
            def _():
                k = turn - z
                slot = lax.rem(k, pairs)
                up_copy(k, d).wait_recv()
                line_send[k, d] = (acc[slot, d] + up_recv[k, d].astype(jnp.float32)).astype(jnp.bfloat16)
                up_copy(k, d).start()
            g = e - 1
            @pl.when((z < pairs - 1) & (z > g) & (turn >= down_lag) & (turn < lines + down_lag))
            def _():
                k = turn - down_lag
                slot = lax.rem(k, pairs)
                down_copy(k, g).wait_recv()
                line_send[k, g] = (acc[slot, g] + down_recv[k, g].astype(jnp.float32)).astype(jnp.bfloat16)
                down_copy(k, g).start()

        for v in range(2 * early):
            @pl.when(turn == v + pairs - 1)
            def _():
                finish(v, v // 2, v % pairs)
                if v % 2 == 0:
                    pair_send[v // 2] = mat[v // 2].astype(jnp.bfloat16)
                    pair_copy(v // 2).start()

        @pl.when(turn >= 2 * early + pairs - 1)
        def _():
            v = turn - (pairs - 1)
            finish(v, v - early, lax.rem(v, pairs))
            add_norm(v - early)

        return carry

    lax.fori_loop(0, lines + pairs - 1, step, 0)

    for c in range(early):
        pair_copy(c).wait_recv()
        mat[c] = mat[c] + pair_recv[c].astype(jnp.float32)
        add_norm(c)

    half = COLOURS * colblk
    norm[:half, :] = 1.0 / (mass_ref[...] + norm[:half, :] + norm[half:, :])

    def fresh_copy(turn, face):
        return pltpu.make_async_remote_copy(
            src_ref=fresh.at[turn], dst_ref=face_recv.at[turn, face ^ 1], send_sem=fresh_ssem.at[turn, face],
            recv_sem=face_rsem.at[turn, face ^ 1], device_id=near_by[face][1], device_id_type=MESH,
        )

    def face_wait(turn, face):
        pltpu.make_async_remote_copy(
            src_ref=fresh.at[turn], dst_ref=face_recv.at[turn, face], send_sem=fresh_ssem.at[turn, face],
            recv_sem=face_rsem.at[turn, face], device_id=near_by[face][1], device_id_type=MESH,
        ).wait_recv()

    last = SWEEPS * COLOURS - 1
    for turn in range(last + 1):
        colour = turn % COLOURS
        low = colour * colblk
        part = slice(low, low + colblk)
        own = state[part, :]
        resid = load_ref[part, :] - mass_ref[part, :] * own
        if turn > 0:
            for face in range(4):
                for r in range(colblk):
                    seen[face, r:r + 1, :] = near[face, pl.ds(faces_ref[face, low + r], 1), :]
            sides = [own] + [seen[face] for face in range(4)]
            for k in range(chunks):
                for h in range(cols // 128):
                    total = None
                    for s in range(5):
                        at = (colour * 5 + s) * colblk
                        term = mat[k, at:at + colblk, h * 128:(h + 1) * 128] * sides[s]
                        total = term if total is None else total + term
                    at = k * cols + h * 128
                    prod[:, at:at + 128] = split(total)
            applied = jnp.dot(prod[...], spread[...], preferred_element_type=jnp.float32)
            resid = resid - (applied[:colblk] + applied[colblk:])
        value = own + resid * norm[part, :]
        state[part, :] = value
        if turn < last:
            fresh[turn] = value
            for face in range(4):
                @pl.when(near_by[face][0])
                def _():
                    fresh_copy(turn, face).start()
            for face in range(4):
                @pl.when(near_by[face][0])
                def _():
                    face_wait(turn, face)
                    near[face, part, :] = face_recv[turn, face]
    out_ref[...] = state[...]

    for turn in range(last):
        for face in range(4):
            @pl.when(near_by[face][0])
            def _():
                fresh_copy(turn, face).wait_send()

    def drain_far(k, carry):
        far_copy(k).wait_send()
        return carry

    lax.fori_loop(early, chunks, drain_far, 0)
    for c in range(early):
        pair_copy(c).wait_send()

    def drain(k, carry):
        for d in range(pairs):
            @pl.when(z < d)
            def _():
                up_copy(k, d).wait_send()

            @pl.when(z > d)
            def _():
                down_copy(k, d).wait_send()
        return carry

    lax.fori_loop(0, lines, drain, 0)


def fused(tiles, owner, target, mass, rhs, faces):
    count, width = tiles.shape[1:]
    rowblk = mass.shape[1] // BLK
    colblk = rowblk // COLOURS
    peers = lax.axis_size("dev")
    pairs = peers // 2
    slots = rowblk * 5
    cols = 256
    chunks = width // cols
    early = chunks // 8
    dest = owner.reshape(1, count)
    row, side = target // 5, target % 5
    place = ((row // colblk) * 5 + side) * colblk + row % colblk
    key = (dest // 2) * slots + place
    right = dest % 2

    def twice(value):
        value = value.reshape(rowblk, BLK)
        return jnp.concatenate([value, value], axis=1)

    vmem = pl.BlockSpec(memory_space=pltpu.VMEM)
    steps = SWEEPS * COLOURS - 1
    out = pl.pallas_call(
        functools.partial(assemble_and_smooth, pairs, cols, early, (lax.axis_size("grp"), peers)),
        out_shape=jax.ShapeDtypeStruct((rowblk, 2 * BLK), jnp.float32),
        in_specs=[pl.BlockSpec(memory_space=pl.ANY), vmem, vmem, vmem, vmem, pl.BlockSpec(memory_space=pltpu.SMEM)],
        out_specs=vmem,
        scratch_shapes=[
            pltpu.VMEM((chunks, count, cols), jnp.bfloat16),
            pltpu.VMEM((pairs * slots, count), jnp.bfloat16),
            pltpu.VMEM((pairs * slots, count), jnp.bfloat16),
            pltpu.VMEM((chunks, pairs * slots, cols), jnp.bfloat16),
            pltpu.VMEM((chunks, pairs * slots, cols), jnp.bfloat16),
            pltpu.VMEM((pairs, pairs, slots, cols), jnp.float32),
            pltpu.VMEM((chunks + early, pairs, slots, cols), jnp.bfloat16),
            pltpu.VMEM((chunks + early, pairs, slots, cols), jnp.bfloat16),
            pltpu.VMEM((chunks + early, pairs, slots, cols), jnp.bfloat16),
            pltpu.VMEM((early, slots, cols), jnp.bfloat16),
            pltpu.VMEM((early, slots, cols), jnp.bfloat16),
            pltpu.VMEM((width, 2 * BLK), jnp.bfloat16),
            pltpu.VMEM((chunks, slots, cols), jnp.float32),
            pltpu.VMEM((2 * rowblk, 2 * BLK), jnp.float32),
            pltpu.VMEM((rowblk, 2 * BLK), jnp.float32),
            pltpu.VMEM((4, rowblk, 2 * BLK), jnp.float32),
            pltpu.VMEM((4, colblk, 2 * BLK), jnp.float32),
            pltpu.VMEM((2 * colblk, width), jnp.bfloat16),
            pltpu.VMEM((steps, colblk, 2 * BLK), jnp.float32),
            pltpu.VMEM((steps, 4, colblk, 2 * BLK), jnp.float32),
            pltpu.SemaphoreType.DMA((chunks,)),
            pltpu.SemaphoreType.DMA((chunks,)),
            pltpu.SemaphoreType.DMA((chunks,)),
            pltpu.SemaphoreType.DMA((chunks + early, pairs)),
            pltpu.SemaphoreType.DMA((chunks + early, pairs)),
            pltpu.SemaphoreType.DMA((chunks + early, pairs)),
            pltpu.SemaphoreType.DMA((steps, 4)),
            pltpu.SemaphoreType.DMA((steps, 4)),
            pltpu.SemaphoreType.DMA((early,)),
            pltpu.SemaphoreType.DMA((early,)),
        ],
        compiler_params=pltpu.CompilerParams(
            collective_id=0, has_side_effects=True, vmem_limit_bytes=58 * 1024 * 1024
        ),
    )(tiles, key, right, twice(mass), twice(rhs), faces[:, 0, :])
    return out[:, :BLK].reshape(1, -1)


def solution(mesh):
    placed = (
        P("grp", "dev", None),
        P("grp", "dev", None),
        P("grp", "dev"),
        P("grp", "dev"),
        P("grp", "dev"),
        P(None, "grp", "dev"),
    )
    peers = mesh.shape["dev"]
    return jax.shard_map(
        fused if peers % 2 == 0 and peers <= 8 else body,
        mesh=mesh, in_specs=placed, out_specs=P("grp", "dev"), check_vma=False,
    )
```

```python
import functools

import jax
import jax.numpy as jnp
from jax import lax
from jax.experimental import pallas as pl
from jax.experimental.pallas import tpu as pltpu
from jax.sharding import PartitionSpec as P

BLK = 64
COLOURS = 4
SWEEPS = 2
MESH = pl.DeviceIdType.MESH


def padded(array, sides, width):
    for axis, dim in sides:
        peers, length = (lax.axis_size(axis), array.shape[dim])
        up = [(i, (i + 1) % peers) for i in range(peers - 1)]
        down = [(j, i) for i, j in up]
        last = lax.slice_in_dim(array, length - width, length, axis=dim)
        leading = lax.slice_in_dim(array, 0, width, axis=dim)
        before = lax.ppermute(last, axis, up)
        after = lax.ppermute(leading, axis, down)
        array = jnp.concatenate([before, array, after], axis=dim)
    return array


def share(fresh):
    grid = padded(fresh.reshape(1, 1, -1), (("grp", 0), ("dev", 1)), 1)
    return jnp.stack([grid[1, 0], grid[1, 2], grid[0, 1], grid[2, 1]]).reshape(
        4, fresh.shape[0], fresh.shape[1]
    )


def pack_slots(tiles_dev, aim, where_to, peers, slots, keep):
    width = tiles_dev.shape[1]
    place = jnp.where(keep, where_to, peers * slots)
    packed = jnp.zeros((peers * slots, width), jnp.bfloat16).at[place].set(tiles_dev, mode="drop")
    labels = jnp.full((peers * slots,), -1, jnp.int32).at[place].set(aim, mode="drop")
    return (packed.reshape(peers, slots, width), labels.reshape(peers, slots))


def add_tiles(got, got_labels, slots_dev):
    width = got.shape[2]
    picks = (got_labels.reshape(1, -1) == lax.iota(jnp.int32, slots_dev)[:, None]).astype(
        jnp.bfloat16
    )
    return jnp.dot(picks, got.reshape(-1, width), preferred_element_type=jnp.float32)


def body(tiles, owner, target, mass, rhs, faces):
    count = tiles.shape[1]
    rowblk = mass.shape[1] // BLK
    colblk = rowblk // COLOURS
    peers = lax.axis_size("dev")
    slots_dev = rowblk * 5
    dest = owner[0, :, 0]
    aim = target[0]
    cap = max(2, 2 * count // peers)
    member = (dest[:, None] == lax.iota(jnp.int32, peers)[None, :]).astype(jnp.int32)
    order = jnp.sum((jnp.cumsum(member, axis=0) - 1) * member, axis=1)
    packed, labels = pack_slots(tiles[0], aim, dest * cap + order, peers, cap, order >= 0)
    got, got_labels = (
        lax.all_to_all(packed, "dev", split_axis=0, concat_axis=0, tiled=True),
        lax.all_to_all(labels, "dev", split_axis=0, concat_axis=0, tiled=True),
    )
    assembled = add_tiles(got, got_labels, slots_dev)
    blocks = assembled.reshape(rowblk, 5, BLK, BLK)
    scale = mass.reshape(rowblk, BLK)
    load = rhs.reshape(rowblk, BLK)
    links = faces[:, 0, :]
    denom = scale + jnp.sum(jnp.abs(blocks), axis=(1, 3))
    state = jnp.zeros((rowblk, BLK), jnp.float32)
    nearby = jnp.zeros((4, rowblk, BLK), jnp.float32)
    high = lax.Precision.HIGHEST
    for sweep in range(SWEEPS):
        for colour in range(COLOURS):
            low = colour * colblk
            upper = low + colblk
            seen = jnp.stack(
                [jnp.take(nearby[face], links[face, low:upper], axis=0) for face in range(4)],
                axis=1,
            )
            own = state[low:upper]
            applied = jnp.einsum("rij,rj->ri", blocks[low:upper, 0], own, precision=high)
            applied = applied + jnp.einsum(
                "rfij,rfj->ri", blocks[low:upper, 1:], seen, precision=high
            )
            resid = load[low:upper] - scale[low:upper] * own - applied
            state = state.at[low:upper].set(own + resid / denom[low:upper])
            if sweep + 1 < SWEEPS or colour + 1 < COLOURS:
                nearby = nearby.at[:, low:upper].set(share(state[low:upper]))
    return state.reshape(1, -1)

def assemble_and_smooth(pairs, cols, early, names, tiles_hbm, key_ref, right_ref, mass_in, load_in, faces_ref, out_ref,
                        tiles_v, pick_far, pick_own, far_send, far_recv, acc, line_send, up_recv, down_recv, pair_send, pair_recv,
                        spread, mat, norm, state, near, seen, prod, fresh, face_recv,
                        tile_sem, far_ssem, far_rsem, line_ssem, up_rsem, down_rsem, fresh_ssem, face_rsem, pair_ssem, pair_rsem, mass_ref, load_ref):
    grp = lax.axis_index("grp")
    dev = lax.axis_index("dev")
    n_grp, n_dev = names
    z = dev // 2
    x = dev % 2
    chunks = tiles_v.shape[0]
    lines = chunks + early
    slots = mat.shape[1]
    colblk = slots // (5 * COLOURS)
    near_by = [
        (dev >= 1, {"dev": dev - 1}),
        (dev < n_dev - 1, {"dev": dev + 1}),
        (grp >= 1, {"grp": grp - 1}),
        (grp < n_grp - 1, {"grp": grp + 1}),
    ]
    partners = near_by + [(dev >= 2, {"dev": dev - 2}), (dev < n_dev - 2, {"dev": dev + 2})]

    def load_tiles(k):
        return pltpu.make_async_copy(
            tiles_hbm.at[0, :, pl.ds(pl.multiple_of(k * cols, cols), cols)], tiles_v.at[k], tile_sem.at[k]
        )

    for k in range(chunks):
        load_tiles(k).start()

    barrier = pltpu.get_barrier_semaphore()
    for there, who in partners:
        @pl.when(there)
        def _():
            pl.semaphore_signal(barrier, inc=1, device_id=who, device_id_type=MESH)

    key = key_ref[...]
    right = right_ref[...]
    key_far = jnp.where(right != x, key, -1)
    key_own = jnp.where(right == x, key, -1)
    rows = lax.broadcasted_iota(jnp.int32, (slots, key.shape[1]), 0)
    for d in range(pairs):
        part = slice(d * slots, (d + 1) * slots)
        pick_far[part, :] = jnp.where(rows + d * slots == key_far, 1.0, 0.0).astype(jnp.bfloat16)

    pl.semaphore_wait(barrier, sum(there.astype(jnp.int32) for there, who in partners))

    def far_copy(k):
        return pltpu.make_async_remote_copy(
            src_ref=far_send.at[k], dst_ref=far_recv.at[k], send_sem=far_ssem.at[k], recv_sem=far_rsem.at[k],
            device_id={"dev": z * 2 + 1 - x}, device_id_type=MESH,
        )

    def pair_copy(c):
        return pltpu.make_async_remote_copy(
            src_ref=pair_send.at[c], dst_ref=pair_recv.at[c], send_sem=pair_ssem.at[c], recv_sem=pair_rsem.at[c],
            device_id={"dev": z * 2 + 1 - x}, device_id_type=MESH,
        )

    def up_copy(k, d):
        return pltpu.make_async_remote_copy(
            src_ref=line_send.at[k, d], dst_ref=up_recv.at[k, d], send_sem=line_ssem.at[k, d],
            recv_sem=up_rsem.at[k, d], device_id={"dev": dev + 2}, device_id_type=MESH,
        )

    def down_copy(k, d):
        return pltpu.make_async_remote_copy(
            src_ref=line_send.at[k, d], dst_ref=down_recv.at[k, d], send_sem=line_ssem.at[k, d],
            recv_sem=down_rsem.at[k, d], device_id={"dev": dev - 2}, device_id_type=MESH,
        )

    def send_far(k, carry):
        load_tiles(k).wait()
        for d in range(pairs):
            part = slice(d * slots, (d + 1) * slots)
            far_send[k, part, :] = jnp.dot(
                pick_far[part, :], tiles_v[k], preferred_element_type=jnp.float32
            ).astype(jnp.bfloat16)
        far_copy(k).start()
        return carry

    for c in range(early):
        load_tiles(c).wait()
    lax.fori_loop(early, chunks, send_far, 0)

    for d in range(pairs):
        part = slice(d * slots, (d + 1) * slots)
        pick_own[part, :] = jnp.where(rows + d * slots == key_own, 1.0, 0.0).astype(jnp.bfloat16)
    lane = lax.broadcasted_iota(jnp.int32, (cols, 128), 0) // BLK
    unit = lax.broadcasted_iota(jnp.int32, (cols, 128), 1) % BLK
    for k in range(chunks):
        spread[k * cols:(k + 1) * cols, :] = jnp.where(lane + k * (cols // BLK) == unit, 1.0, 0.0).astype(jnp.bfloat16)
    for r in range(mass_ref.shape[0]):
        for flat, wide in ((mass_in, mass_ref), (load_in, load_ref)):
            value = flat[:, r * BLK:(r + 1) * BLK]
            wide[r:r + 1, :] = jnp.concatenate([value, value], axis=1)
    norm[...] = jnp.zeros_like(norm)
    near[...] = jnp.zeros_like(near)
    state[...] = jnp.zeros_like(state)

    def split(value):
        top = value.astype(jnp.bfloat16).astype(jnp.float32)
        return jnp.concatenate([top, value - top], axis=0).astype(jnp.bfloat16)

    def finish(v, k, slot):
        mat[k] = acc[slot, z]

        @pl.when(z > 0)
        def _():
            up_copy(v, z).wait_recv()
            mat[k] = mat[k] + up_recv[v, z].astype(jnp.float32)

        @pl.when(z < pairs - 1)
        def _():
            down_copy(v, z).wait_recv()
            mat[k] = mat[k] + down_recv[v, z].astype(jnp.float32)

    def add_norm(k):
        size = jnp.abs(mat[k]).reshape(COLOURS, 5, colblk, cols)
        size = jnp.sum(size, axis=1).reshape(COLOURS * colblk, cols)
        at = k * cols if isinstance(k, int) else pl.multiple_of(k * cols, cols)
        norm[...] += jnp.dot(split(size), spread[pl.ds(at, cols), :], preferred_element_type=jnp.float32)

    def step(turn, carry):
        for v in range(2 * early):
            @pl.when(turn == v)
            def _():
                pick = pick_own if v % 2 else pick_far
                for d in range(pairs):
                    acc[v % pairs, d] = jnp.dot(
                        pick[d * slots:(d + 1) * slots, :], tiles_v[v // 2], preferred_element_type=jnp.float32
                    )

        @pl.when((turn >= 2 * early) & (turn < lines))
        def _():
            k = turn - early
            slot = lax.rem(turn, pairs)
            far_copy(k).wait_recv()
            for d in range(pairs):
                part = slice(d * slots, (d + 1) * slots)
                acc[slot, d] = jnp.dot(
                    pick_own[part, :], tiles_v[k], preferred_element_type=jnp.float32
                ) + far_recv[k, part, :].astype(jnp.float32)

        @pl.when(turn < lines)
        def _():
            k = turn
            slot = lax.rem(k, pairs)
            for d in reversed(range(1, pairs)):
                @pl.when(z == 0)
                def _():
                    line_send[k, d] = acc[slot, d].astype(jnp.bfloat16)
                    up_copy(k, d).start()
            for d in range(pairs - 1):
                @pl.when(z == pairs - 1)
                def _():
                    line_send[k, d] = acc[slot, d].astype(jnp.bfloat16)
                    down_copy(k, d).start()

        down_lag = pairs - 1 - z
        for e in range(1, pairs):
            d = pairs - e
            @pl.when((z > 0) & (z < d) & (turn >= z) & (turn < lines + z))
            def _():
                k = turn - z
                slot = lax.rem(k, pairs)
                up_copy(k, d).wait_recv()
                line_send[k, d] = (acc[slot, d] + up_recv[k, d].astype(jnp.float32)).astype(jnp.bfloat16)
                up_copy(k, d).start()
            g = e - 1
            @pl.when((z < pairs - 1) & (z > g) & (turn >= down_lag) & (turn < lines + down_lag))
            def _():
                k = turn - down_lag
                slot = lax.rem(k, pairs)
                down_copy(k, g).wait_recv()
                line_send[k, g] = (acc[slot, g] + down_recv[k, g].astype(jnp.float32)).astype(jnp.bfloat16)
                down_copy(k, g).start()

        for v in range(2 * early):
            @pl.when(turn == v + pairs - 1)
            def _():
                finish(v, v // 2, v % pairs)
                if v % 2 == 0:
                    pair_send[v // 2] = mat[v // 2].astype(jnp.bfloat16)
                    pair_copy(v // 2).start()

        @pl.when(turn >= 2 * early + pairs - 1)
        def _():
            v = turn - (pairs - 1)
            finish(v, v - early, lax.rem(v, pairs))
            add_norm(v - early)

        return carry

    lax.fori_loop(0, lines + pairs - 1, step, 0)

    for c in range(early):
        pair_copy(c).wait_recv()
        mat[c] = mat[c] + pair_recv[c].astype(jnp.float32)
        add_norm(c)

    half = COLOURS * colblk
    norm[:half, :] = 1.0 / (mass_ref[...] + norm[:half, :] + norm[half:, :])

    def fresh_copy(turn, face):
        return pltpu.make_async_remote_copy(
            src_ref=fresh.at[turn], dst_ref=face_recv.at[turn, face ^ 1], send_sem=fresh_ssem.at[turn, face],
            recv_sem=face_rsem.at[turn, face ^ 1], device_id=near_by[face][1], device_id_type=MESH,
        )

    def face_wait(turn, face):
        pltpu.make_async_remote_copy(
            src_ref=fresh.at[turn], dst_ref=face_recv.at[turn, face], send_sem=fresh_ssem.at[turn, face],
            recv_sem=face_rsem.at[turn, face], device_id=near_by[face][1], device_id_type=MESH,
        ).wait_recv()

    last = SWEEPS * COLOURS - 1
    for turn in range(last + 1):
        colour = turn % COLOURS
        low = colour * colblk
        part = slice(low, low + colblk)
        own = state[part, :]
        resid = load_ref[part, :] - mass_ref[part, :] * own
        if turn > 0:
            for face in range(4):
                for r in range(colblk):
                    seen[face, r:r + 1, :] = near[face, pl.ds(faces_ref[face, low + r], 1), :]
            sides = [own] + [seen[face] for face in range(4)]
            for k in range(chunks):
                for h in range(cols // 128):
                    total = None
                    for s in range(5):
                        at = (colour * 5 + s) * colblk
                        term = mat[k, at:at + colblk, h * 128:(h + 1) * 128] * sides[s]
                        total = term if total is None else total + term
                    at = k * cols + h * 128
                    prod[:, at:at + 128] = split(total)
            applied = jnp.dot(prod[...], spread[...], preferred_element_type=jnp.float32)
            resid = resid - (applied[:colblk] + applied[colblk:])
        value = own + resid * norm[part, :]
        state[part, :] = value
        if turn < last:
            fresh[turn] = value
            for face in range(4):
                @pl.when(near_by[face][0])
                def _():
                    fresh_copy(turn, face).start()
            for face in range(4):
                @pl.when(near_by[face][0])
                def _():
                    face_wait(turn, face)
                    near[face, part, :] = face_recv[turn, face]
    out_ref[...] = state[...]

    for turn in range(last):
        for face in range(4):
            @pl.when(near_by[face][0])
            def _():
                fresh_copy(turn, face).wait_send()

    def drain_far(k, carry):
        far_copy(k).wait_send()
        return carry

    lax.fori_loop(early, chunks, drain_far, 0)
    for c in range(early):
        pair_copy(c).wait_send()

    def drain(k, carry):
        for d in range(pairs):
            @pl.when(z < d)
            def _():
                up_copy(k, d).wait_send()

            @pl.when(z > d)
            def _():
                down_copy(k, d).wait_send()
        return carry

    lax.fori_loop(0, lines, drain, 0)


def fused(tiles, owner, target, mass, rhs, faces):
    count, width = tiles.shape[1:]
    rowblk = mass.shape[1] // BLK
    colblk = rowblk // COLOURS
    peers = lax.axis_size("dev")
    pairs = peers // 2
    slots = rowblk * 5
    cols = 256
    chunks = width // cols
    early = chunks // 8
    dest = owner.reshape(1, count)
    row, side = target // 5, target % 5
    place = ((row // colblk) * 5 + side) * colblk + row % colblk
    key = (dest // 2) * slots + place
    right = dest % 2

    vmem = pl.BlockSpec(memory_space=pltpu.VMEM)
    steps = SWEEPS * COLOURS - 1
    out = pl.pallas_call(
        functools.partial(assemble_and_smooth, pairs, cols, early, (lax.axis_size("grp"), peers)),
        out_shape=jax.ShapeDtypeStruct((rowblk, 2 * BLK), jnp.float32),
        in_specs=[pl.BlockSpec(memory_space=pl.ANY), vmem, vmem, vmem, vmem, pl.BlockSpec(memory_space=pltpu.SMEM)],
        out_specs=vmem,
        scratch_shapes=[
            pltpu.VMEM((chunks, count, cols), jnp.bfloat16),
            pltpu.VMEM((pairs * slots, count), jnp.bfloat16),
            pltpu.VMEM((pairs * slots, count), jnp.bfloat16),
            pltpu.VMEM((chunks, pairs * slots, cols), jnp.bfloat16),
            pltpu.VMEM((chunks, pairs * slots, cols), jnp.bfloat16),
            pltpu.VMEM((pairs, pairs, slots, cols), jnp.float32),
            pltpu.VMEM((chunks + early, pairs, slots, cols), jnp.bfloat16),
            pltpu.VMEM((chunks + early, pairs, slots, cols), jnp.bfloat16),
            pltpu.VMEM((chunks + early, pairs, slots, cols), jnp.bfloat16),
            pltpu.VMEM((early, slots, cols), jnp.bfloat16),
            pltpu.VMEM((early, slots, cols), jnp.bfloat16),
            pltpu.VMEM((width, 2 * BLK), jnp.bfloat16),
            pltpu.VMEM((chunks, slots, cols), jnp.float32),
            pltpu.VMEM((2 * rowblk, 2 * BLK), jnp.float32),
            pltpu.VMEM((rowblk, 2 * BLK), jnp.float32),
            pltpu.VMEM((4, rowblk, 2 * BLK), jnp.float32),
            pltpu.VMEM((4, colblk, 2 * BLK), jnp.float32),
            pltpu.VMEM((2 * colblk, width), jnp.bfloat16),
            pltpu.VMEM((steps, colblk, 2 * BLK), jnp.float32),
            pltpu.VMEM((steps, 4, colblk, 2 * BLK), jnp.float32),
            pltpu.SemaphoreType.DMA((chunks,)),
            pltpu.SemaphoreType.DMA((chunks,)),
            pltpu.SemaphoreType.DMA((chunks,)),
            pltpu.SemaphoreType.DMA((chunks + early, pairs)),
            pltpu.SemaphoreType.DMA((chunks + early, pairs)),
            pltpu.SemaphoreType.DMA((chunks + early, pairs)),
            pltpu.SemaphoreType.DMA((steps, 4)),
            pltpu.SemaphoreType.DMA((steps, 4)),
            pltpu.SemaphoreType.DMA((early,)),
            pltpu.SemaphoreType.DMA((early,)),
            pltpu.VMEM((rowblk, 2 * BLK), jnp.float32),
            pltpu.VMEM((rowblk, 2 * BLK), jnp.float32),
        ],
        compiler_params=pltpu.CompilerParams(
            collective_id=0, has_side_effects=True, vmem_limit_bytes=58 * 1024 * 1024
        ),
    )(tiles, key, right, mass, rhs, faces[:, 0, :])
    return out[:, :BLK].reshape(1, -1)


def solution(mesh):
    placed = (
        P("grp", "dev", None),
        P("grp", "dev", None),
        P("grp", "dev"),
        P("grp", "dev"),
        P("grp", "dev"),
        P(None, "grp", "dev"),
    )
    peers = mesh.shape["dev"]
    return jax.shard_map(
        fused if peers % 2 == 0 and peers <= 8 else body,
        mesh=mesh, in_specs=placed, out_specs=P("grp", "dev"), check_vma=False,
    )
```
